32 devices in a mesh: group: 2 (over y), shard: 16 (over z, x, core).
Axes of the slice: x: 2, y: 2, z: 4, core: 2. Of those that a mesh axis runs over, the one named last changes fastest.
Arguments:
- item_features: bfloat16 [4096, 1024], P(('group', 'shard')), may hold values from -6 to 6
- tower_weight: bfloat16 [1024, 1024], replicated, may hold values from -0.1875 to 0.1875
- item_table: bfloat16 [4096, 1024], P(('group', 'shard')), may hold values from -4 to 4
- owner: int32 [4096, 1], P(('group', 'shard')), may hold values from 0 to 15; in each aligned block of 128 rows (0 to 127, 128 to 255, ...) at most 16 rows name the same one
- table_slot: int32 [4096], P(('group', 'shard')), may hold values from 0 to 127
- pair_users: int32 [4096, 2], P(('group', 'shard')), may hold values from 0 to 63
- user_comps: bfloat16 [128, 1024], P(('group', 'shard')), may hold values from -0.5 to 0.5
- user_gates: bfloat16 [128, 64], P(('group', 'shard')), may hold values from -6 to 6
Outputs:
- tower_grad: float32 [1024, 1024], P('shard')
- table_grad: float32 [4096, 1024], P(('group', 'shard'))
- user_comp_grad: float32 [128, 1024], P(('group', 'shard'))
- user_gate_grad: float32 [128, 64], P(('group', 'shard'))
The draws below stay inside these ranges and needn't reach their ends.
Inputs may be any that keep to these rules, and one draw needn't show every extreme that they name: Among the rows of one device, no owner is named more than 16 times, a bound that some block reaches. `pair_users`: user numbers within the item's own group.
All inputs are finite; a program needn't handle non-finite values.
Results may differ from the reference program's by a relative error of at most 0.0042.
Values may be sent and summed in bfloat16 or wider, within the bound.
No kernel may reach another device: no remote copies, remote signals or barrier semaphores. Data moves between devices by JAX's collectives and lax.ppermute only.
A program may use at most 64 MiB of HBM per device.

```python
import math
import jax
import jax.numpy as jnp
import numpy as np
from jax import lax

COMPS = 8
D = 1024
ITEM_DEV = 128
TABLE_DEV = 128
CAP = 16
USERS_G = 64
ITEMS = 4096
TABLE = 4096
USERS = 128
N_GROUP = 2
N_SHARD = 16


def touch_ends(values, stream_key, low, top_value):
    spot = [jax.random.randint(jax.random.fold_in(stream_key, axis), (), 0, length) for axis, length in enumerate(values.shape)]
    main_axis = values.shape.index(max(values.shape))
    beside = spot[:main_axis] + [(spot[main_axis] + 1) % values.shape[main_axis]] + spot[main_axis + 1:]
    return values.at[tuple(spot)].set(low).at[tuple(beside)].set(top_value)


def strengthened(drawn, stream_key, source, target, parts, factor):
    def block_of(dim):
        return (jnp.arange(drawn.shape[dim]) // (drawn.shape[dim] // parts)).reshape((-1,) + (1,) * (drawn.ndim - 1 - dim))

    first = jax.random.permutation(stream_key, parts)[block_of(target)]
    far = (block_of(target) + parts // 2) % parts
    return jnp.where((block_of(source) == first) | (block_of(source) == far), factor * drawn, drawn)


def level_of(own_key, extent, split, low, high):
    gain, own = 1.0, jax.random.fold_in(own_key, 6)
    for dim, blocks in split:
        heights = jnp.exp(jax.random.uniform(jax.random.fold_in(own, dim), (blocks,), jnp.float32, low / len(split), high / len(split)))
        gain = gain * jnp.repeat(heights, extent[dim] // blocks).reshape([-1 if axis == dim else 1 for axis in range(len(extent))])
    return gain


def deal_out(own_key, own, number, rows, number_of, top, reach, skew):
    ranking = jax.random.permutation(own_key, number_of)
    packed, common = shares(number_of, rows * top, reach, skew, True), shares(number_of, rows * top, reach, skew, False)
    places = jnp.arange(number_of)

    def named(tallies, turn):
        used = int((tallies > 0).sum())
        fixed = max(1, used // 4)
        moved = fixed + (places - fixed + turn * (used - fixed)) % max(1, number_of - fixed)
        return jnp.zeros((number_of,), jnp.int32).at[ranking[jnp.where(places < fixed, places, moved)]].set(jnp.asarray(tallies, jnp.int32))

    tallies = jnp.where(number % 4 == 0, named(packed, number // 4), named(common, number - number // 4 - 1))
    mixed = jax.random.permutation(jax.random.fold_in(own, 3), number_of)
    giver, sink = mixed[0:number_of // 2 * 2:2], mixed[1:number_of // 2 * 2:2]
    room = jnp.minimum(tallies[giver] - 1, reach - tallies[sink]) // 2
    room = jnp.where((giver == ranking[0]) | (sink == ranking[0]) | (tallies[sink] == 0), 0, jnp.maximum(room, 0))
    moved = jax.random.randint(jax.random.fold_in(own, 4), (number_of // 2,), 0, 1 << 20) % (room + 1)
    tallies = tallies.at[giver].add(-moved).at[sink].add(moved)
    items = jnp.searchsorted(jnp.cumsum(tallies), jnp.arange(rows * top), side="right").astype(jnp.int32)
    listing = items.reshape(top, rows).T
    listing = listing[jax.random.permutation(jax.random.fold_in(own, 1), rows)]
    turn = jax.random.randint(jax.random.fold_in(own, 2), (rows, 1), 0, top)
    return jnp.take_along_axis(listing, (jnp.arange(top)[None, :] + turn) % top, axis=1)


def shares(count, total, bound, skew, full):
    loads = [(1 << 20) // math.isqrt(grade ** skew) + 1 for grade in range(1, count + 1)]
    largest = bound if full else min(bound, max(-(-total // count), total * loads[0] // sum(loads)))
    least = 1 if total - largest >= count - 1 else 0
    counts, surplus = [largest] + [least] * (count - 1), total - largest - least * (count - 1)
    while surplus > 0:
        candidates = [i for i in range(1, count) if counts[i] < largest] or [i for i in range(1, count) if counts[i] < bound]
        mass, left = sum([loads[i] for i in candidates]), surplus
        for i in candidates:
            extra = min(bound - counts[i], max(1, left * loads[i] // mass), surplus)
            counts[i] = counts[i] + extra
            surplus = surplus - extra
    return np.array(counts)


def centred(rng, extent, width, limit, shards=(), kind=jnp.bfloat16):
    drawn = width * jax.random.normal(rng, extent, jnp.float32)
    if shards:
        drawn = drawn * level_of(rng, extent, shards, -0.22, 0.18)
    return jnp.clip(drawn, -limit, limit).astype(kind)


def gaussian_with(own_key, shape, scale, reach, split, heavy, dtype=jnp.bfloat16):
    array = scale * jax.random.normal(own_key, shape, jnp.float32)
    if split:
        array = array * level_of(own_key, shape, split, -0.22, 0.18)
    return jnp.clip(strengthened(array, jax.random.fold_in(own_key, 3), *heavy), -reach, reach).astype(dtype)


def setup_inputs(seed: int = 0) -> dict:
    key_of = jax.random.split(jax.random.key(seed), 9)
    item_features = gaussian_with(key_of[0], (ITEMS, D), 1.0, 6.0, ((0, 32),), (0, 1, 32, 2.75))
    tower_weight = centred(key_of[1], (D, D), D ** -0.5, 0.1875)
    item_table = centred(key_of[2], (TABLE, D), 0.6, 4.0, ((0, 32),))
    owner_keys = jax.random.split(jax.random.fold_in(key_of[3], 1), ITEMS // ITEM_DEV)
    owner_turns = jax.random.permutation(jax.random.fold_in(key_of[3], 3), ITEMS // ITEM_DEV)
    owner = jax.vmap(lambda own, number: deal_out(jax.random.fold_in(key_of[3], 2), own, number, ITEM_DEV, N_SHARD, 1, CAP, 2))(owner_keys, owner_turns).reshape((ITEMS, 1))
    table_slot = touch_ends(jax.random.randint(key_of[4], (ITEMS,), 0, TABLE_DEV), jax.random.fold_in(key_of[4], 1), 0, TABLE_DEV - 1).astype(jnp.int32)
    pair_users = touch_ends(jax.random.randint(key_of[5], (ITEMS, 2), 0, USERS_G), jax.random.fold_in(key_of[5], 1), 0, USERS_G - 1).astype(jnp.int32)
    user_comps = centred(key_of[6], (USERS, D), 0.09, 0.5, ((0, 32),))
    user_gates = centred(key_of[7], (USERS, COMPS * COMPS), 1.5, 6.0, ((0, 32),))
    return dict(item_features=item_features, tower_weight=tower_weight, item_table=item_table, owner=owner, table_slot=table_slot, pair_users=pair_users, user_comps=user_comps, user_gates=user_gates)


highest = lax.Precision.HIGHEST

def exact_gelu(values):
    return jax.nn.gelu(values, approximate=False)

def mixture_score(normed, users, gates):
    rows_here = normed.shape[0]
    logits = jnp.einsum('npk,nqk->npq', users, normed, precision=highest)
    weights = jax.nn.sigmoid(gates.reshape(rows_here, COMPS, COMPS) + logits)
    return 0.125 * lax.optimization_barrier(jnp.sum(weights * logits, axis=(1, 2)))

def pair_loss(embedded, table_rows, pos_users, neg_users, pos_gates, neg_gates, present):
    rows_here = embedded.shape[0]
    combined = (embedded + table_rows).reshape(rows_here, COMPS, -1)
    normed = combined * lax.rsqrt(lax.optimization_barrier(jnp.mean(combined * combined, axis=-1, keepdims=True)) + 1e-06)
    pos_score = mixture_score(normed, pos_users.reshape(rows_here, COMPS, -1), pos_gates)
    neg_score = mixture_score(normed, neg_users.reshape(rows_here, COMPS, -1), neg_gates)
    return jnp.sum(present * (jax.nn.softplus(-pos_score) + jax.nn.softplus(neg_score)))

def reference(item_features, tower_weight, item_table, owner, table_slot, pair_users, user_comps, user_gates):
    group_items = ITEM_DEV * N_SHARD
    group_table = TABLE_DEV * N_SHARD
    gate_width = COMPS * COMPS

    def one_group(carry, stacked):
        features, targets, slot_ids, pairs, table, users, gates = stacked
        preact = jnp.dot(features, tower_weight, preferred_element_type=jnp.float32)
        gelu_value, gelu_back = jax.vjp(exact_gelu, preact)
        embedded = lax.optimization_barrier(gelu_value.astype(jnp.bfloat16)).astype(jnp.float32)
        table_index = (targets[:, 0] * TABLE_DEV + slot_ids).astype(jnp.int32)
        pos_ids = pairs[:, 0]
        neg_ids = pairs[:, 1]
        table_rows = table[table_index].astype(jnp.float32)
        pos_users = users[pos_ids].astype(jnp.float32)
        neg_users = users[neg_ids].astype(jnp.float32)
        pos_gates = gates[pos_ids].astype(jnp.float32)
        neg_gates = gates[neg_ids].astype(jnp.float32)
        present = jnp.ones((group_items,), jnp.float32)
        derivs = jax.grad(pair_loss, argnums=(0, 1, 2, 3, 4, 5))(embedded, table_rows, pos_users, neg_users, pos_gates, neg_gates, present)
        table_grad = jnp.zeros((group_table, D), jnp.float32).at[table_index].add(derivs[1])
        user_grad = jnp.zeros((USERS_G, D), jnp.float32).at[pos_ids].add(derivs[2]).at[neg_ids].add(derivs[3])
        gate_grad = jnp.zeros((USERS_G, gate_width), jnp.float32).at[pos_ids].add(derivs[4]).at[neg_ids].add(derivs[5])
        rounded = lax.optimization_barrier(derivs[0].astype(jnp.bfloat16)).astype(jnp.float32)
        d_preact = gelu_back(rounded)[0].astype(jnp.bfloat16)
        carry = carry + lax.dot_general(features, d_preact, (((0,), (0,)), ((), ())), preferred_element_type=jnp.float32)
        return (carry, (table_grad, user_grad, gate_grad))
    stacked = (item_features.reshape(N_GROUP, group_items, D), owner.reshape(N_GROUP, group_items, 1), table_slot.reshape(N_GROUP, group_items), pair_users.reshape(N_GROUP, group_items, 2), item_table.reshape(N_GROUP, group_table, D), user_comps.reshape(N_GROUP, USERS_G, D), user_gates.reshape(N_GROUP, USERS_G, gate_width))
    tower_grad, outputs = lax.scan(one_group, jnp.zeros((D, D), jnp.float32), stacked)
    table_grads, user_grads, gate_grads = outputs
    return (tower_grad, table_grads.reshape(-1, D), user_grads.reshape(-1, D), gate_grads.reshape(-1, gate_width))
```

```python
import functools
import math

import jax
import jax.numpy as jnp
import numpy as np
from jax import lax
from jax.experimental import pallas as pl
from jax.experimental.pallas import tpu as pltpu
from jax.sharding import Mesh, PartitionSpec as P

COMPS = 8
KINDS = 4
LANES = 128
F32 = jnp.float32
BF16 = jnp.bfloat16
VMEM_LIMIT = 48 * 1024 * 1024


def iota(shape, axis):
    return lax.broadcasted_iota(jnp.int32, shape, axis)


def split_by(numbers, size):
    quotient = jnp.floor((numbers.astype(F32) + 0.5) * (1.0 / size)).astype(jnp.int32)
    return quotient, numbers - quotient * size


def nn(a, b):
    return lax.dot_general(a, b, (((1,), (0,)), ((), ())), preferred_element_type=F32)


def nt(a, b):
    return lax.dot_general(a, b, (((1,), (1,)), ((), ())), preferred_element_type=F32)


def halves(values):
    high = values.astype(BF16)
    return high, (values - high.astype(F32)).astype(BF16)


def erf(x):
    x = jnp.clip(x, -3.832506856900711, 3.832506856900711)
    s = x * x
    top = 0.00022905065861350646
    for c in (0.0034082910107109506, 0.050955695062380861, 0.18520832239976145, 1.128379143519084):
        top = top * s + c
    low = -1.1791602954361697e-7
    for c in (
        0.000023547966471313185,
        0.0010179625278914885,
        0.014070470171167667,
        0.11098505178285362,
        0.49746925110067538,
        1.0,
    ):
        low = low * s + c
    return x * top / low


def pack_kernel(cap, block, x_ref, owner_ref, slot_ref, pair_ref, user_ref, gate_ref, out_ref):
    items = x_ref.shape[0]
    rows = out_ref.shape[0]
    held = user_ref.shape[0]
    wide = (items, items)
    own_i = jnp.broadcast_to(owner_ref[...].astype(F32), wide)
    own_j = jnp.transpose(own_i)
    i, j = iota(wide, 0), iota(wide, 1)
    same = own_i == own_j
    rank_row = jnp.sum(jnp.where(same & (i < j), 1.0, 0.0), axis=0, keepdims=True)
    rank_col = jnp.sum(jnp.where(same & (j < i), 1.0, 0.0), axis=1, keepdims=True)
    slot_col = jnp.sum(
        jnp.where(i == j, jnp.broadcast_to(slot_ref[...].astype(F32), wide), 0.0), axis=1, keepdims=True
    )
    own_row = own_j[0:1, :]
    row_ids = iota((rows, items), 0)
    place = (own_row * block + rank_row).astype(jnp.int32)
    select = (row_ids == place).astype(F32).astype(BF16)
    _, spot = split_by(iota((rows, held), 0), block)
    lane = iota((rows, held), 1)
    main = nn(select, x_ref[...]) + nn(
        (spot == lane + cap).astype(F32).astype(BF16), user_ref[...]
    )
    width = gate_ref.shape[1]
    padded = nn(
        gate_ref[...], (iota((width, LANES), 0) == iota((width, LANES), 1)).astype(F32).astype(BF16)
    ).astype(BF16)
    gates = nn((spot == lane + cap + held).astype(F32).astype(BF16), padded)
    kind, turn = split_by(iota((items, LANES), 1), cap)
    pairs = pair_ref[...].astype(F32)
    value = jnp.where(
        kind == 0,
        slot_col,
        jnp.where(kind == 1, pairs[:, 0:1], jnp.where(kind == 2, pairs[:, 1:2], 1.0)),
    )
    value = jnp.where((kind < KINDS) & (rank_col.astype(jnp.int32) == turn), value, 0.0)
    to_owner = row_ids == (own_row * block + (cap + held)).astype(jnp.int32)
    header = nn(to_owner.astype(F32).astype(BF16), value.astype(BF16))
    out_ref[:, :LANES] = (main[:, :LANES] + gates).astype(BF16)
    out_ref[:, LANES : 2 * LANES] = (main[:, LANES : 2 * LANES] + header).astype(BF16)
    out_ref[:, 2 * LANES :] = main[:, 2 * LANES :].astype(BF16)


def train_kernel(
    shards, cap, block, held, order,
    recv_ref, wt_ref, table_t_ref,
    table_grad_ref, user_ref, xt_ref, dpt_ref,
    comp_ref, pos_ref, neg_ref, dpos_ref, dneg_ref, norm_ref, pre_ref, scale_ref,
):
    rows, width = recv_ref.shape
    slots = shards * cap
    users = shards * held
    comps = COMPS
    size = width // comps
    tables = table_t_ref.shape[1]
    recv = recv_ref[...]

    def rows_of(count, per, first):
        quotient, rest = split_by(iota((count, rows), 0), per)
        picked = iota((count, rows), 1) == quotient * block + first + rest
        return picked.astype(F32).astype(BF16)

    x_rows = nn(rows_of(slots, cap, 0), recv)
    x_t = jnp.transpose(x_rows).astype(BF16)
    unit = width // shards
    for place, first in enumerate(order):
        xt_ref[place * unit : (place + 1) * unit, :] = x_t[first * unit : (first + 1) * unit, :]
    user_rows = nn(rows_of(users, held, cap), recv)
    for p in range(comps):
        comp_ref[pl.ds(p, users, stride=comps), :] = user_rows[:, p * size : (p + 1) * size]
    comp_rows = comp_ref[...].astype(BF16)
    comp_t = jnp.transpose(comp_ref[...]).astype(BF16)
    gates_t = jnp.transpose(nn(rows_of(users, held, cap + held), recv[:, :LANES]))[: comps * comps]
    pairs = (comps * comps, comps * comps)
    outer, inner = split_by(iota(pairs, 0), comps)
    swap = (iota(pairs, 1) == inner * comps + outer).astype(F32).astype(BF16)
    gates_t = nn(swap, gates_t.astype(BF16)).astype(BF16)

    raw = nn(rows_of(shards, 1, cap + held), recv[:, LANES : 2 * LANES])
    source, turn = split_by(iota((shards, slots), 1), cap)
    spread = (source == iota((shards, slots), 0)).astype(F32).astype(BF16)
    fields = nn(jnp.transpose(raw).astype(BF16), spread)
    kind, field_turn = split_by(iota((LANES, slots), 0), cap)
    _, slot_turn = split_by(iota((LANES, slots), 1), cap)
    fields = jnp.where(field_turn == slot_turn, fields, 0.0)

    def field(number):
        return jnp.sum(jnp.where(kind == number, fields, 0.0), axis=0, keepdims=True)

    table_row = field(0).astype(jnp.int32)
    pos_row = field(1).astype(jnp.int32)
    neg_row = field(2).astype(jnp.int32)
    present = field(3)
    pick_table = (iota((tables, slots), 0) == table_row).astype(F32).astype(BF16)
    user_ids = iota((users, slots), 0)
    gate_pos = nn(gates_t, (user_ids == pos_row).astype(F32).astype(BF16))
    gate_neg = nn(gates_t, (user_ids == neg_row).astype(F32).astype(BF16))
    comp_twice = jnp.concatenate([comp_rows, comp_rows], axis=1)
    ids3 = iota((users, comps, slots), 0)
    is_pos = ids3 == pos_row[None]
    is_neg = ids3 == neg_row[None]

    for q in range(comps):
        part = slice(q * size, (q + 1) * size)
        pre = nn(wt_ref[part, :], x_t)
        pre_ref[part, :] = pre
        embedded = (0.5 * pre * (1.0 + erf(pre * math.sqrt(0.5)))).astype(BF16).astype(F32)
        combined = embedded + nn(table_t_ref[part, :], pick_table)
        scale = lax.rsqrt(jnp.mean(combined * combined, axis=0, keepdims=True) + 1e-06)
        scale_ref[q : q + 1, :] = scale
        normed = combined * scale
        norm_ref[part, :] = normed
        high, low = halves(normed)
        logits = nn(comp_twice, jnp.concatenate([high, low], axis=0))
        logits = logits.reshape(users, comps, slots)
        pos_ref[q * comps : (q + 1) * comps, :] = jnp.sum(jnp.where(is_pos, logits, 0.0), axis=0)
        neg_ref[q * comps : (q + 1) * comps, :] = jnp.sum(jnp.where(is_neg, logits, 0.0), axis=0)

    def side(logits, gates, sign):
        weights = jax.nn.sigmoid(gates + logits)
        score = 0.125 * jnp.sum(weights * logits, axis=0, keepdims=True)
        d_score = 0.125 * sign * jax.nn.sigmoid(sign * score) * present
        d_gates = d_score * (logits * weights * (1.0 - weights))
        return d_gates + d_score * weights, d_gates

    d_pos, dg_pos = side(pos_ref[...], gate_pos, -1.0)
    d_neg, dg_neg = side(neg_ref[...], gate_neg, 1.0)
    dpos_ref[...] = d_pos
    dneg_ref[...] = d_neg

    pad = -(-held // 8) * 8
    mate, rest = split_by(iota((shards * pad, slots), 0), pad)
    person = jnp.where(rest < held, mate * held + rest, -1)
    mask_pos = (person == pos_row).astype(F32).astype(BF16)
    mask_neg = (person == neg_row).astype(F32).astype(BF16)
    d_gate = jnp.zeros((shards * pad, comps * comps), F32)
    for mask, values in ((mask_pos, dg_pos), (mask_neg, dg_neg)):
        for piece in halves(values):
            d_gate = d_gate + nt(mask, nn(swap, piece).astype(BF16))
    own = held * comps
    user_ref[:, own:, : comps * comps] = d_gate.reshape(shards, pad, comps * comps)
    user_ref[:, own:, comps * comps :] = jnp.zeros(
        (shards, pad, size - comps * comps), F32
    )

    d_users = jnp.zeros((users * comps, size), F32)
    for q in range(comps):
        part = slice(q * size, (q + 1) * size)
        d_logit_pos = dpos_ref[q * comps : (q + 1) * comps, :][None]
        d_logit_neg = dneg_ref[q * comps : (q + 1) * comps, :][None]
        dense = jnp.where(is_pos, d_logit_pos, 0.0) + jnp.where(is_neg, d_logit_neg, 0.0)
        dense_high, dense_low = halves(dense.reshape(users * comps, slots))
        normed = norm_ref[part, :]
        high, low = halves(normed)
        d_users = d_users + nt(dense_high, high) + nt(dense_high, low) + nt(dense_low, high)
        d_normed = nn(comp_t, dense_high) + nn(comp_t, dense_low)
        inner = jnp.mean(d_normed * normed, axis=0, keepdims=True)
        d_combined = scale_ref[q : q + 1, :] * (d_normed - normed * inner)
        total = jnp.zeros((tables, size), F32)
        for piece in halves(d_combined):
            total = total + nt(pick_table, piece)
        table_grad_ref[:, part] = total
        pre = pre_ref[part, :]
        slope = 0.5 * (1.0 + erf(pre * math.sqrt(0.5))) + pre * (
            jnp.exp(-0.5 * pre * pre) * (1.0 / math.sqrt(2.0 * math.pi))
        )
        dpt_ref[part, :] = (d_combined.astype(BF16).astype(F32) * slope).astype(BF16)
    user_ref[:, :own, :] = d_users.reshape(shards, own, size)


def tower_kernel(groups, x_ref, x_far_ref, d_ref, d_far_ref, out_ref):
    wide = d_ref.shape[0] // groups
    for g in range(groups):
        part = slice(g * wide, (g + 1) * wide)
        out_ref[g] = (
            nt(x_ref[...], d_ref[part, :]) + nt(x_far_ref[...], d_far_ref[part, :])
        ).astype(BF16)


def local(
    sizes, item_features, tower_weight, item_table, owner, table_slot, pair_users, user_comps, user_gates
):
    groups, deep, across, cores = sizes
    shards = deep * across * cores
    shard_axes = ("z", "x", "core")
    items, width = item_features.shape
    cap = max(1, 2 * items // shards)
    held = user_comps.shape[0]
    block = -(-(cap + 2 * held) // 8) * 8
    rows = shards * block
    slots = shards * cap
    size = width // COMPS
    users = shards * held
    params = pltpu.CompilerParams(vmem_limit_bytes=VMEM_LIMIT)

    packed = pl.pallas_call(
        functools.partial(pack_kernel, cap, block),
        out_shape=jax.ShapeDtypeStruct((rows, width), BF16),
        compiler_params=params,
        name="pack",
    )(item_features, owner, table_slot.reshape(1, items), pair_users, user_comps, user_gates)
    recv = lax.all_to_all(packed, shard_axes, split_axis=0, concat_axis=0, tiled=True)
    weight_t = tower_weight.T
    table_t = item_table.T

    order = [
        (z * across + x) * cores + c for c in range(cores) for x in range(across) for z in range(deep)
    ]
    own = held * COMPS
    pad = -(-held // 8) * 8
    table_grad, user_part, x_t, dp_t = pl.pallas_call(
        functools.partial(train_kernel, shards, cap, block, held, order),
        out_shape=(
            jax.ShapeDtypeStruct((item_table.shape[0], width), F32),
            jax.ShapeDtypeStruct((shards, own + pad, size), F32),
            jax.ShapeDtypeStruct((width, slots), BF16),
            jax.ShapeDtypeStruct((width, slots), BF16),
        ),
        scratch_shapes=[
            pltpu.VMEM((users * COMPS, size), F32),
            pltpu.VMEM((COMPS * COMPS, slots), F32),
            pltpu.VMEM((COMPS * COMPS, slots), F32),
            pltpu.VMEM((COMPS * COMPS, slots), F32),
            pltpu.VMEM((COMPS * COMPS, slots), F32),
            pltpu.VMEM((width, slots), F32),
            pltpu.VMEM((width, slots), F32),
            pltpu.VMEM((COMPS, slots), F32),
        ],
        compiler_params=params,
        name="train",
    )(recv, weight_t, table_t)

    core = lax.axis_index("core")
    half = width // cores
    swap = [(0, 1), (1, 0)]
    x_own = lax.dynamic_slice_in_dim(x_t, core * half, half, 0)
    x_far = lax.ppermute(lax.dynamic_slice_in_dim(x_t, (1 - core) * half, half, 0), "core", swap)
    dp_far = lax.ppermute(dp_t, "core", swap)
    part = pl.pallas_call(
        functools.partial(tower_kernel, groups),
        out_shape=jax.ShapeDtypeStruct((groups, half, width // groups), BF16),
        compiler_params=params,
        name="tower",
    )(x_own, x_far, dp_t, dp_far)
    wide = width // groups
    got = lax.all_to_all(
        part.reshape(groups * across, half // across, wide), ("y", "x"), split_axis=0, concat_axis=0, tiled=True
    )
    summed = jnp.sum(got.astype(F32), axis=0).astype(BF16)
    got = lax.all_to_all(
        summed.reshape(deep, half // across // deep, wide), "z", split_axis=0, concat_axis=0, tiled=True
    )
    mine = jnp.sum(got.astype(F32), axis=0)
    if groups == 2:
        other = lax.ppermute(mine, "y", swap)
        first = lax.axis_index("y") == 0
        tower_grad = jnp.concatenate(
            [jnp.where(first, mine, other), jnp.where(first, other, mine)], axis=1
        )
    else:
        tower_grad = lax.all_gather(mine, "y", axis=1, tiled=True)

    got_users = lax.all_to_all(user_part, shard_axes, split_axis=0, concat_axis=0, tiled=True)
    user_sum = jnp.sum(got_users, axis=0)
    user_comp_grad = user_sum[:own].reshape(held, width)
    user_gate_grad = user_sum[own : own + held, : COMPS * COMPS]
    return tower_grad, table_grad, user_comp_grad, user_gate_grad


def solution(mesh):
    groups, shards = mesh.shape["group"], mesh.shape["shard"]
    cores = 2
    chips = shards // cores
    across = 1
    while 8 * across * across <= chips:
        across *= 2
    sizes = (groups, chips // across, across, cores)
    fine = Mesh(np.asarray(mesh.devices).reshape(sizes), ("y", "z", "x", "core"))
    whole = ("y", "z", "x", "core")
    placed = (
        P(whole, None), P(), P(whole, None), P(whole, None),
        P(whole), P(whole, None), P(whole, None), P(whole, None),
    )
    return jax.shard_map(
        functools.partial(local, sizes),
        mesh=fine,
        in_specs=placed,
        out_specs=(
            P(("z", "x", "core"), None), P(whole, None), P(whole, None), P(whole, None),
        ),
        check_vma=False,
    )
```

```python
import functools
import math

import jax
import jax.numpy as jnp
import numpy as np
from jax import lax
from jax.experimental import pallas as pl
from jax.experimental.pallas import tpu as pltpu
from jax.sharding import Mesh, PartitionSpec as P

COMPS = 8
KINDS = 4
LANES = 128
F32 = jnp.float32
BF16 = jnp.bfloat16
VMEM_LIMIT = 48 * 1024 * 1024
PACK_LIMIT = 60 * 1024 * 1024
FEW = 4


def iota(shape, axis):
    return lax.broadcasted_iota(jnp.int32, shape, axis)


def split_by(numbers, size):
    quotient = jnp.floor((numbers.astype(F32) + 0.5) * (1.0 / size)).astype(jnp.int32)
    return quotient, numbers - quotient * size


def nn(a, b):
    return lax.dot_general(a, b, (((1,), (0,)), ((), ())), preferred_element_type=F32)


def nt(a, b):
    return lax.dot_general(a, b, (((1,), (1,)), ((), ())), preferred_element_type=F32)


def halves(values):
    high = values.astype(BF16)
    return high, (values - high.astype(F32)).astype(BF16)


def erf(x):
    x = jnp.clip(x, -3.832506856900711, 3.832506856900711)
    s = x * x
    top = 0.00022905065861350646
    for c in (0.0034082910107109506, 0.050955695062380861, 0.18520832239976145, 1.128379143519084):
        top = top * s + c
    low = -1.1791602954361697e-7
    for c in (
        0.000023547966471313185,
        0.0010179625278914885,
        0.014070470171167667,
        0.11098505178285362,
        0.49746925110067538,
        1.0,
    ):
        low = low * s + c
    return x * top / low


def pack_kernel(cap, block, x_ref, owner_ref, slot_ref, pair_ref, user_ref, gate_ref, out_ref):
    items = x_ref.shape[0]
    rows = out_ref.shape[0]
    held = user_ref.shape[0]
    wide = (items, items)
    own_j = jnp.broadcast_to(owner_ref[...].astype(F32), wide)
    own_i = jnp.transpose(own_j)
    i, j = iota(wide, 0), iota(wide, 1)
    same = own_i == own_j
    rank_row = jnp.sum(jnp.where(same & (i < j), 1.0, 0.0), axis=0, keepdims=True)
    rank_col = jnp.sum(jnp.where(same & (j < i), 1.0, 0.0), axis=1, keepdims=True)

    def column(row):
        return jnp.sum(jnp.where(i == j, row.astype(F32), 0.0), axis=1, keepdims=True)

    slot_col = column(slot_ref[...])
    first_col, second_col = column(pair_ref[0:1, :]), column(pair_ref[1:2, :])
    own_row = own_j[0:1, :]
    row_ids = iota((rows, items), 0)
    place = (own_row * block + rank_row).astype(jnp.int32)
    select = (row_ids == place).astype(F32).astype(BF16)
    _, spot = split_by(iota((rows, held), 0), block)
    lane = iota((rows, held), 1)
    main = nn(select, x_ref[...]) + nn(
        (spot == lane + cap).astype(F32).astype(BF16), user_ref[...]
    )
    width = gate_ref.shape[1]
    padded = nn(
        gate_ref[...], (iota((width, LANES), 0) == iota((width, LANES), 1)).astype(F32).astype(BF16)
    ).astype(BF16)
    gates = nn((spot == lane + cap + held).astype(F32).astype(BF16), padded)
    kind, turn = split_by(iota((items, LANES), 1), cap)
    value = jnp.where(
        kind == 0,
        slot_col,
        jnp.where(kind == 1, first_col, jnp.where(kind == 2, second_col, 1.0)),
    )
    value = jnp.where((kind < KINDS) & (rank_col.astype(jnp.int32) == turn), value, 0.0)
    to_owner = row_ids == (own_row * block + (cap + held)).astype(jnp.int32)
    header = nn(to_owner.astype(F32).astype(BF16), value.astype(BF16))
    out_ref[:, :LANES] = (main[:, :LANES] + gates).astype(BF16)
    out_ref[:, LANES : 2 * LANES] = (main[:, LANES : 2 * LANES] + header).astype(BF16)
    out_ref[:, 2 * LANES :] = main[:, 2 * LANES :].astype(BF16)


def train_kernel(
    shards, cap, block, held, order,
    core_ref, recv_ref, wt_ref, table_t_ref,
    table_grad_ref, user_ref, x_own_ref, x_far_ref, dpt_ref,
    comp_ref, pos_ref, neg_ref, dpos_ref, dneg_ref, norm_ref, pre_ref, scale_ref,
):
    rows, width = recv_ref.shape
    slots = shards * cap
    users = shards * held
    comps = COMPS
    size = width // comps
    tables = table_t_ref.shape[1]
    recv = recv_ref[...]

    def rows_of(count, per, first):
        quotient, rest = split_by(iota((count, rows), 0), per)
        picked = iota((count, rows), 1) == quotient * block + first + rest
        return picked.astype(F32).astype(BF16)

    x_rows = nn(rows_of(slots, cap, 0), recv)
    x_t = jnp.transpose(x_rows).astype(BF16)
    unit = width // shards
    first_core = core_ref[0] == 0
    for place, (here, there) in enumerate(order):
        into = slice(place * unit, (place + 1) * unit)
        one = x_t[here * unit : (here + 1) * unit, :]
        two = x_t[there * unit : (there + 1) * unit, :]
        x_own_ref[into, :] = jnp.where(first_core, one, two)
        x_far_ref[into, :] = jnp.where(first_core, two, one)
    user_rows = nn(rows_of(users, held, cap), recv)
    for p in range(comps):
        comp_ref[pl.ds(p, users, stride=comps), :] = user_rows[:, p * size : (p + 1) * size]
    comp_rows = comp_ref[...].astype(BF16)
    comp_t = jnp.transpose(comp_ref[...]).astype(BF16)
    gates_t = jnp.transpose(nn(rows_of(users, held, cap + held), recv[:, :LANES]))[: comps * comps]
    pairs = (comps * comps, comps * comps)
    outer, inner = split_by(iota(pairs, 0), comps)
    swap = (iota(pairs, 1) == inner * comps + outer).astype(F32).astype(BF16)
    gates_t = nn(swap, gates_t.astype(BF16)).astype(BF16)

    raw = nn(rows_of(shards, 1, cap + held), recv[:, LANES : 2 * LANES])
    source, turn = split_by(iota((shards, slots), 1), cap)
    spread = (source == iota((shards, slots), 0)).astype(F32).astype(BF16)
    fields = nn(jnp.transpose(raw).astype(BF16), spread)
    kind, field_turn = split_by(iota((LANES, slots), 0), cap)
    _, slot_turn = split_by(iota((LANES, slots), 1), cap)
    fields = jnp.where(field_turn == slot_turn, fields, 0.0)

    def field(number):
        return jnp.sum(jnp.where(kind == number, fields, 0.0), axis=0, keepdims=True)

    table_row = field(0).astype(jnp.int32)
    pos_row = field(1).astype(jnp.int32)
    neg_row = field(2).astype(jnp.int32)
    present = field(3)
    pick_table = (iota((tables, slots), 0) == table_row).astype(F32).astype(BF16)
    user_ids = iota((users, slots), 0)
    gate_pos = nn(gates_t, (user_ids == pos_row).astype(F32).astype(BF16))
    gate_neg = nn(gates_t, (user_ids == neg_row).astype(F32).astype(BF16))
    comp_twice = jnp.concatenate([comp_rows, comp_rows], axis=1)
    ids3 = iota((users, comps, slots), 0)
    is_pos = ids3 == pos_row[None]
    is_neg = ids3 == neg_row[None]

    for q in range(comps):
        part = slice(q * size, (q + 1) * size)
        pre = nn(wt_ref[part, :], x_t)
        pre_ref[part, :] = pre
        embedded = (0.5 * pre * (1.0 + erf(pre * math.sqrt(0.5)))).astype(BF16).astype(F32)
        combined = embedded + nn(table_t_ref[part, :], pick_table)
        scale = lax.rsqrt(jnp.mean(combined * combined, axis=0, keepdims=True) + 1e-06)
        scale_ref[q : q + 1, :] = scale
        normed = combined * scale
        norm_ref[part, :] = normed
        high, low = halves(normed)
        logits = nn(comp_twice, jnp.concatenate([high, low], axis=0))
        logits = logits.reshape(users, comps, slots)
        pos_ref[q * comps : (q + 1) * comps, :] = jnp.sum(jnp.where(is_pos, logits, 0.0), axis=0)
        neg_ref[q * comps : (q + 1) * comps, :] = jnp.sum(jnp.where(is_neg, logits, 0.0), axis=0)

    def side(logits, gates, sign):
        weights = jax.nn.sigmoid(gates + logits)
        score = 0.125 * jnp.sum(weights * logits, axis=0, keepdims=True)
        d_score = 0.125 * sign * jax.nn.sigmoid(sign * score) * present
        d_gates = d_score * (logits * weights * (1.0 - weights))
        return d_gates + d_score * weights, d_gates

    d_pos, dg_pos = side(pos_ref[...], gate_pos, -1.0)
    d_neg, dg_neg = side(neg_ref[...], gate_neg, 1.0)
    dpos_ref[...] = d_pos
    dneg_ref[...] = d_neg

    pad = -(-held // 8) * 8
    mate, rest = split_by(iota((shards * pad, slots), 0), pad)
    person = jnp.where(rest < held, mate * held + rest, -1)
    mask_pos = (person == pos_row).astype(F32).astype(BF16)
    mask_neg = (person == neg_row).astype(F32).astype(BF16)
    d_gate = jnp.zeros((shards * pad, comps * comps), F32)
    for mask, values in ((mask_pos, dg_pos), (mask_neg, dg_neg)):
        for piece in halves(values):
            d_gate = d_gate + nt(mask, nn(swap, piece).astype(BF16))
    own = held * comps
    user_ref[:, own:, : comps * comps] = d_gate.reshape(shards, pad, comps * comps)
    user_ref[:, own:, comps * comps :] = jnp.zeros(
        (shards, pad, size - comps * comps), F32
    )

    d_users = jnp.zeros((users * comps, size), F32)
    for q in range(comps):
        part = slice(q * size, (q + 1) * size)
        d_logit_pos = dpos_ref[q * comps : (q + 1) * comps, :][None]
        d_logit_neg = dneg_ref[q * comps : (q + 1) * comps, :][None]
        dense = jnp.where(is_pos, d_logit_pos, 0.0) + jnp.where(is_neg, d_logit_neg, 0.0)
        dense_high, dense_low = halves(dense.reshape(users * comps, slots))
        normed = norm_ref[part, :]
        high, low = halves(normed)
        d_users = d_users + nt(dense_high, high) + nt(dense_high, low) + nt(dense_low, high)
        d_normed = nn(comp_t, dense_high) + nn(comp_t, dense_low)
        inner = jnp.mean(d_normed * normed, axis=0, keepdims=True)
        d_combined = scale_ref[q : q + 1, :] * (d_normed - normed * inner)
        total = jnp.zeros((tables, size), F32)
        for piece in halves(d_combined):
            total = total + nt(pick_table, piece)
        table_grad_ref[:, part] = total
        pre = pre_ref[part, :]
        slope = 0.5 * (1.0 + erf(pre * math.sqrt(0.5))) + pre * (
            jnp.exp(-0.5 * pre * pre) * (1.0 / math.sqrt(2.0 * math.pi))
        )
        dpt_ref[part, :] = (d_combined.astype(BF16).astype(F32) * slope).astype(BF16)
    user_ref[:, :own, :] = d_users.reshape(shards, own, size)


def views(refs, count):
    return list(refs) if len(refs) == count else [refs[0].at[k] for k in range(count)]


def blocks(count, shape):
    if count <= FEW:
        return [jax.ShapeDtypeStruct(shape, BF16)] * count
    return [jax.ShapeDtypeStruct((count,) + shape, BF16)]


def partner_of(me_ref, k, count):
    return me_ref[0] ^ k if count <= FEW else k


def exchange(parts, axis, count):
    if count > FEW:
        return [lax.all_to_all(parts[0], axis, split_axis=0, concat_axis=0, tiled=True)]
    return [parts[0]] + [
        lax.ppermute(parts[k], axis, [(i, i ^ k) for i in range(count)]) for k in range(1, count)
    ]


def tower_kernel(groups, across, me_ref, x_ref, x_far_ref, d_ref, d_far_ref, *outs):
    wide = d_ref.shape[0] // groups
    tall = x_ref.shape[0] // across
    count = groups * across
    for k, out_ref in enumerate(views(outs, count)):
        partner = partner_of(me_ref, k, count)
        tower_rows = pl.ds(pl.multiple_of(lax.rem(partner, across) * tall, tall), tall)
        columns = pl.ds(pl.multiple_of(lax.div(partner, across) * wide, wide), wide)
        out_ref[...] = (
            nt(x_ref[tower_rows, :], d_ref[columns, :]) + nt(x_far_ref[tower_rows, :], d_far_ref[columns, :])
        ).astype(BF16)


def sum_kernel(given, count, deep, me_ref, *refs):
    ins, outs = views(refs[:given], count), views(refs[given:], deep)
    tall = outs[0].shape[0]
    for k, out_ref in enumerate(outs):
        part = pl.ds(pl.multiple_of(partner_of(me_ref, k, deep) * tall, tall), tall)
        total = ins[0][part, :].astype(F32)
        for in_ref in ins[1:]:
            total = total + in_ref[part, :].astype(F32)
        out_ref[...] = total.astype(BF16)


def local(
    sizes, item_features, tower_weight, item_table, owner, table_slot, pair_users, user_comps, user_gates
):
    groups, deep, across, cores = sizes
    shards = deep * across * cores
    shard_axes = ("z", "x", "core")
    items, width = item_features.shape
    cap = max(1, 2 * items // shards)
    held = user_comps.shape[0]
    block = -(-(cap + 2 * held) // 8) * 8
    rows = shards * block
    slots = shards * cap
    size = width // COMPS
    users = shards * held
    params = pltpu.CompilerParams(vmem_limit_bytes=VMEM_LIMIT)

    packed = pl.pallas_call(
        functools.partial(pack_kernel, cap, block),
        out_shape=jax.ShapeDtypeStruct((rows, width), BF16),
        compiler_params=pltpu.CompilerParams(vmem_limit_bytes=PACK_LIMIT),
        name="pack",
    )(item_features, owner.T, table_slot.reshape(1, items), pair_users.T, user_comps, user_gates)
    recv = lax.all_to_all(packed, shard_axes, split_axis=0, concat_axis=0, tiled=True)
    weight_t = tower_weight.T
    table_t = item_table.T

    order = [
        ((z * across + x) * cores, (z * across + x) * cores + 1) for x in range(across) for z in range(deep)
    ]
    half = width // cores
    core = lax.axis_index("core")
    scalar = pl.BlockSpec(memory_space=pltpu.SMEM)
    vmem = pl.BlockSpec(memory_space=pltpu.VMEM)
    own = held * COMPS
    pad = -(-held // 8) * 8
    table_grad, user_part, x_own, x_send, dp_t = pl.pallas_call(
        functools.partial(train_kernel, shards, cap, block, held, order),
        out_shape=(
            jax.ShapeDtypeStruct((item_table.shape[0], width), F32),
            jax.ShapeDtypeStruct((shards, own + pad, size), F32),
            jax.ShapeDtypeStruct((half, slots), BF16),
            jax.ShapeDtypeStruct((half, slots), BF16),
            jax.ShapeDtypeStruct((width, slots), BF16),
        ),
        in_specs=[scalar, vmem, vmem, vmem],
        scratch_shapes=[
            pltpu.VMEM((users * COMPS, size), F32),
            pltpu.VMEM((COMPS * COMPS, slots), F32),
            pltpu.VMEM((COMPS * COMPS, slots), F32),
            pltpu.VMEM((COMPS * COMPS, slots), F32),
            pltpu.VMEM((COMPS * COMPS, slots), F32),
            pltpu.VMEM((width, slots), F32),
            pltpu.VMEM((width, slots), F32),
            pltpu.VMEM((COMPS, slots), F32),
        ],
        compiler_params=params,
        name="train",
    )(core.reshape(1), recv, weight_t, table_t)

    swap = [(0, 1), (1, 0)]
    x_far = lax.ppermute(x_send, "core", swap)
    dp_far = lax.ppermute(dp_t, "core", swap)
    partners = groups * across
    tall, wide = half // across, width // groups
    parts = pl.pallas_call(
        functools.partial(tower_kernel, groups, across),
        out_shape=blocks(partners, (tall, wide)),
        in_specs=[scalar] + [vmem] * 4,
        compiler_params=params,
        name="tower",
    )(lax.axis_index(("y", "x")).reshape(1), x_own, x_far, dp_t, dp_far)
    got = exchange(parts, ("y", "x"), partners)
    parts = pl.pallas_call(
        functools.partial(sum_kernel, len(got), partners, deep),
        out_shape=blocks(deep, (tall // deep, wide)),
        in_specs=[scalar] + [vmem] * len(got),
        compiler_params=params,
        name="sums",
    )(lax.axis_index("z").reshape(1), *got)
    got = exchange(parts, "z", deep)
    if deep > FEW:
        mine = jnp.sum(got[0].astype(F32), axis=0)
    else:
        mine = sum(part.astype(F32) for part in got)
    if groups == 2:
        other = lax.ppermute(mine, "y", swap)
        first = lax.axis_index("y") == 0
        tower_grad = jnp.concatenate(
            [jnp.where(first, mine, other), jnp.where(first, other, mine)], axis=1
        )
    else:
        tower_grad = lax.all_gather(mine, "y", axis=1, tiled=True)

    got_users = lax.all_to_all(user_part, shard_axes, split_axis=0, concat_axis=0, tiled=True)
    user_sum = jnp.sum(got_users, axis=0)
    user_comp_grad = user_sum[:own].reshape(held, width)
    user_gate_grad = user_sum[own : own + held, : COMPS * COMPS]
    return tower_grad, table_grad, user_comp_grad, user_gate_grad


def solution(mesh):
    groups, shards = mesh.shape["group"], mesh.shape["shard"]
    cores = 2
    chips = shards // cores
    across = 1
    while 8 * across * across <= chips:
        across *= 2
    sizes = (groups, chips // across, across, cores)
    fine = Mesh(np.asarray(mesh.devices).reshape(sizes), ("y", "z", "x", "core"))
    whole = ("y", "z", "x", "core")
    placed = (
        P(whole, None), P(), P(whole, None), P(whole, None),
        P(whole), P(whole, None), P(whole, None), P(whole, None),
    )
    return jax.shard_map(
        functools.partial(local, sizes),
        mesh=fine,
        in_specs=placed,
        out_specs=(
            P(("z", "x", "core"), None), P(whole, None), P(whole, None), P(whole, None),
        ),
        check_vma=False,
    )
```

```python
import functools
import math

import jax
import jax.numpy as jnp
import numpy as np
from jax import lax
from jax.experimental import pallas as pl
from jax.experimental.pallas import tpu as pltpu
from jax.sharding import Mesh, PartitionSpec as P

COMPS = 8
KINDS = 4
LANES = 128
F32 = jnp.float32
BF16 = jnp.bfloat16
VMEM_LIMIT = 48 * 1024 * 1024
PACK_LIMIT = 60 * 1024 * 1024
FEW = 4


def iota(shape, axis):
    return lax.broadcasted_iota(jnp.int32, shape, axis)


def split_by(numbers, size):
    quotient = jnp.floor((numbers.astype(F32) + 0.5) * (1.0 / size)).astype(jnp.int32)
    return quotient, numbers - quotient * size


def nn(a, b):
    return lax.dot_general(a, b, (((1,), (0,)), ((), ())), preferred_element_type=F32)


def nt(a, b):
    return lax.dot_general(a, b, (((1,), (1,)), ((), ())), preferred_element_type=F32)


def halves(values):
    high = values.astype(BF16)
    return high, (values - high.astype(F32)).astype(BF16)


def erf(x):
    x = jnp.clip(x, -3.832506856900711, 3.832506856900711)
    s = x * x
    top = 0.00022905065861350646
    for c in (0.0034082910107109506, 0.050955695062380861, 0.18520832239976145, 1.128379143519084):
        top = top * s + c
    low = -1.1791602954361697e-7
    for c in (
        0.000023547966471313185,
        0.0010179625278914885,
        0.014070470171167667,
        0.11098505178285362,
        0.49746925110067538,
        1.0,
    ):
        low = low * s + c
    return x * top / low


def pack_kernel(cap, block, x_ref, owner_ref, slot_ref, pair_ref, user_ref, gate_ref, out_ref):
    items = x_ref.shape[0]
    rows = out_ref.shape[0]
    held = user_ref.shape[0]
    wide = (items, items)
    own_j = jnp.broadcast_to(owner_ref[...].astype(F32), wide)
    own_i = jnp.transpose(own_j)
    i, j = iota(wide, 0), iota(wide, 1)
    same = own_i == own_j
    rank_row = jnp.sum(jnp.where(same & (i < j), 1.0, 0.0), axis=0, keepdims=True)
    rank_col = jnp.sum(jnp.where(same & (j < i), 1.0, 0.0), axis=1, keepdims=True)

    def column(row):
        return jnp.sum(jnp.where(i == j, row.astype(F32), 0.0), axis=1, keepdims=True)

    slot_col = column(slot_ref[...])
    first_col, second_col = column(pair_ref[0:1, :]), column(pair_ref[1:2, :])
    own_row = own_j[0:1, :]
    row_ids = iota((rows, items), 0)
    place = (own_row * block + rank_row).astype(jnp.int32)
    select = (row_ids == place).astype(F32).astype(BF16)
    _, spot = split_by(iota((rows, held), 0), block)
    lane = iota((rows, held), 1)
    main = nn(select, x_ref[...]) + nn(
        (spot == lane + cap).astype(F32).astype(BF16), user_ref[...]
    )
    width = gate_ref.shape[1]
    padded = nn(
        gate_ref[...], (iota((width, LANES), 0) == iota((width, LANES), 1)).astype(F32).astype(BF16)
    ).astype(BF16)
    gates = nn((spot == lane + cap + held).astype(F32).astype(BF16), padded)
    kind, turn = split_by(iota((items, LANES), 1), cap)
    value = jnp.where(
        kind == 0,
        slot_col,
        jnp.where(kind == 1, first_col, jnp.where(kind == 2, second_col, 1.0)),
    )
    value = jnp.where((kind < KINDS) & (rank_col.astype(jnp.int32) == turn), value, 0.0)
    to_owner = row_ids == (own_row * block + (cap + held)).astype(jnp.int32)
    header = nn(to_owner.astype(F32).astype(BF16), value.astype(BF16))
    out_ref[:, :LANES] = (main[:, :LANES] + gates).astype(BF16)
    out_ref[:, LANES : 2 * LANES] = (main[:, LANES : 2 * LANES] + header).astype(BF16)
    out_ref[:, 2 * LANES :] = main[:, 2 * LANES :].astype(BF16)


def train_kernel(
    shards, cap, block, held, order,
    core_ref, recv_ref, wt_ref, table_t_ref,
    table_grad_ref, user_ref, x_own_ref, x_far_ref, dpt_ref,
    comp_ref, pos_ref, neg_ref, dpos_ref, dneg_ref, norm_ref, slope_ref, scale_ref,
    split_ref, dense_ref, dc_ref, low_ref,
):
    rows, width = recv_ref.shape
    slots = shards * cap
    users = shards * held
    comps = COMPS
    size = width // comps
    tables = table_t_ref.shape[1]
    recv = recv_ref[...]

    def rows_of(count, per, first):
        quotient, rest = split_by(iota((count, rows), 0), per)
        picked = iota((count, rows), 1) == quotient * block + first + rest
        return picked.astype(F32).astype(BF16)

    picked = nn(jnp.concatenate([rows_of(slots, cap, 0), rows_of(users, held, cap)], axis=0), recv)
    x_t = jnp.transpose(picked[:slots].astype(BF16))
    unit = width // shards
    first_core = core_ref[0] == 0
    for place, (here, there) in enumerate(order):
        into = slice(place * unit, (place + 1) * unit)
        one = x_t[here * unit : (here + 1) * unit, :]
        two = x_t[there * unit : (there + 1) * unit, :]
        x_own_ref[into, :] = jnp.where(first_core, one, two)
        x_far_ref[into, :] = jnp.where(first_core, two, one)
    user_rows = picked[slots:]
    for p in range(comps):
        comp_ref[pl.ds(p, users, stride=comps), :] = user_rows[:, p * size : (p + 1) * size]
    comp_rows = comp_ref[...].astype(BF16)
    comp_t = jnp.transpose(comp_ref[...]).astype(BF16)
    gates_t = jnp.transpose(nn(rows_of(users, held, cap + held), recv[:, :LANES]))[: comps * comps]
    pairs = (comps * comps, comps * comps)
    outer, inner = split_by(iota(pairs, 0), comps)
    swap = (iota(pairs, 1) == inner * comps + outer).astype(F32).astype(BF16)
    gates_t = nn(swap, gates_t.astype(BF16)).astype(BF16)

    raw = nn(rows_of(shards, 1, cap + held), recv[:, LANES : 2 * LANES])
    source, turn = split_by(iota((shards, slots), 1), cap)
    spread = (source == iota((shards, slots), 0)).astype(F32).astype(BF16)
    fields = nn(jnp.transpose(raw).astype(BF16), spread)
    kind, field_turn = split_by(iota((LANES, slots), 0), cap)
    _, slot_turn = split_by(iota((LANES, slots), 1), cap)
    fields = jnp.where(field_turn == slot_turn, fields, 0.0)

    def field(number):
        return jnp.sum(jnp.where(kind == number, fields, 0.0), axis=0, keepdims=True)

    table_row = field(0).astype(jnp.int32)
    pos_row = field(1).astype(jnp.int32)
    neg_row = field(2).astype(jnp.int32)
    present = field(3)
    pick_table = (iota((tables, slots), 0) == table_row).astype(F32).astype(BF16)
    user_ids = iota((users, slots), 0)
    gate_pos = nn(gates_t, (user_ids == pos_row).astype(F32).astype(BF16))
    gate_neg = nn(gates_t, (user_ids == neg_row).astype(F32).astype(BF16))
    comp_twice = jnp.concatenate([comp_rows, comp_rows], axis=1)
    ids3 = iota((users, comps, slots), 0)
    is_pos = ids3 == pos_row[None]
    is_neg = ids3 == neg_row[None]

    slope_ref[...] = nn(wt_ref[...], x_t)
    norm_ref[...] = nn(table_t_ref[...], pick_table)
    for q in range(comps):
        part, wide = slice(q * size, (q + 1) * size), slice(q * slots, (q + 1) * slots)
        pre = slope_ref[part, :]
        share = 0.5 + 0.5 * erf(pre * math.sqrt(0.5))
        slope_ref[part, :] = share + pre * (jnp.exp(-0.5 * pre * pre) * (1.0 / math.sqrt(2.0 * math.pi)))
        combined = (pre * share).astype(BF16).astype(F32) + norm_ref[part, :]
        scale = lax.rsqrt(jnp.mean(combined * combined, axis=0, keepdims=True) + 1e-06)
        scale_ref[q : q + 1, :] = scale
        normed = combined * scale
        norm_ref[part, :] = normed
        high, low = halves(normed)
        split_ref[:size, wide] = high
        split_ref[size:, wide] = low
        logits = nn(comp_twice, split_ref[:, wide]).reshape(users, comps, slots)
        pos_ref[q * comps : (q + 1) * comps, :] = jnp.sum(jnp.where(is_pos, logits, 0.0), axis=0)
        neg_ref[q * comps : (q + 1) * comps, :] = jnp.sum(jnp.where(is_neg, logits, 0.0), axis=0)

    def side(logits, gates, sign):
        weights = jax.nn.sigmoid(gates + logits)
        score = 0.125 * jnp.sum(weights * logits, axis=0, keepdims=True)
        d_score = 0.125 * sign * jax.nn.sigmoid(sign * score) * present
        d_gates = d_score * (logits * weights * (1.0 - weights))
        return d_gates + d_score * weights, d_gates

    d_pos, dg_pos = side(pos_ref[...], gate_pos, -1.0)
    d_neg, dg_neg = side(neg_ref[...], gate_neg, 1.0)
    dpos_ref[...] = d_pos
    dneg_ref[...] = d_neg

    pad = user_ref.shape[1] - held * comps
    mate, rest = split_by(iota((shards * pad, slots), 0), pad)
    person = jnp.where(rest < held, mate * held + rest, -1)
    mask_pos = (person == pos_row).astype(F32).astype(BF16)
    mask_neg = (person == neg_row).astype(F32).astype(BF16)
    d_gate = jnp.zeros((shards * pad, comps * comps), F32)
    for mask, values in ((mask_pos, dg_pos), (mask_neg, dg_neg)):
        for piece in halves(values):
            d_gate = d_gate + nt(mask, nn(swap, piece).astype(BF16))
    own = held * comps
    user_ref[:, own:, : comps * comps] = d_gate.reshape(shards, pad, comps * comps).astype(BF16)
    user_ref[:, own:, comps * comps :] = jnp.zeros(
        (shards, pad, size - comps * comps), BF16
    )

    for q in range(comps):
        wide = slice(q * slots, (q + 1) * slots)
        d_logit_pos = dpos_ref[q * comps : (q + 1) * comps, :][None]
        d_logit_neg = dneg_ref[q * comps : (q + 1) * comps, :][None]
        dense = jnp.where(is_pos, d_logit_pos, 0.0) + jnp.where(is_neg, d_logit_neg, 0.0)
        dense_high, dense_low = halves(dense.reshape(users * comps, slots))
        dense_ref[:, wide] = dense_high
        part = slice(q * size, (q + 1) * size)
        normed = norm_ref[part, :]
        d_normed = nn(comp_t, dense_high) + nn(comp_t, dense_low)
        inner = jnp.mean(d_normed * normed, axis=0, keepdims=True)
        d_combined = scale_ref[q : q + 1, :] * (d_normed - normed * inner)
        d_embedded = d_combined.astype(BF16)
        dpt_ref[part, :] = (d_embedded.astype(F32) * slope_ref[part, :]).astype(BF16)
        dc_ref[part, :] = d_embedded
        low_ref[part, :] = (d_combined - d_embedded.astype(F32)).astype(BF16)
    d_users = nt(dense_ref[...], split_ref[...])
    d_users = d_users[:, :size] + d_users[:, size:]
    user_ref[:, :own, :] = d_users.reshape(shards, own, size).astype(BF16)
    table_grad_ref[...] = nt(pick_table, dc_ref[...]) + nt(pick_table, low_ref[...])


def views(refs, count):
    return list(refs) if len(refs) == count else [refs[0].at[k] for k in range(count)]


def blocks(count, shape):
    if count <= FEW:
        return [jax.ShapeDtypeStruct(shape, BF16)] * count
    return [jax.ShapeDtypeStruct((count,) + shape, BF16)]


def partner_of(me_ref, k, count):
    return me_ref[0] ^ k if count <= FEW else k


def exchange(parts, axis, count):
    if count > FEW:
        return [lax.all_to_all(parts[0], axis, split_axis=0, concat_axis=0, tiled=True)]
    return [parts[0]] + [
        lax.ppermute(parts[k], axis, [(i, i ^ k) for i in range(count)]) for k in range(1, count)
    ]


def tower_kernel(groups, across, me_ref, x_ref, x_far_ref, d_ref, d_far_ref, *outs):
    wide = d_ref.shape[0] // groups
    tall = x_ref.shape[0] // across
    count = groups * across
    for k, out_ref in enumerate(views(outs, count)):
        partner = partner_of(me_ref, k, count)
        tower_rows = pl.ds(pl.multiple_of(lax.rem(partner, across) * tall, tall), tall)
        columns = pl.ds(pl.multiple_of(lax.div(partner, across) * wide, wide), wide)
        out_ref[...] = (
            nt(x_ref[tower_rows, :], d_ref[columns, :]) + nt(x_far_ref[tower_rows, :], d_far_ref[columns, :])
        ).astype(BF16)


def sum_kernel(given, count, deep, me_ref, *refs):
    ins, outs = views(refs[:given], count), views(refs[given:], deep)
    tall = outs[0].shape[0]
    for k, out_ref in enumerate(outs):
        part = pl.ds(pl.multiple_of(partner_of(me_ref, k, deep) * tall, tall), tall)
        total = ins[0][part, :].astype(F32)
        for in_ref in ins[1:]:
            total = total + in_ref[part, :].astype(F32)
        out_ref[...] = total.astype(BF16)


def local(
    sizes, item_features, tower_weight, item_table, owner, table_slot, pair_users, user_comps, user_gates
):
    groups, deep, across, cores = sizes
    shards = deep * across * cores
    shard_axes = ("z", "x", "core")
    items, width = item_features.shape
    cap = max(1, 2 * items // shards)
    held = user_comps.shape[0]
    block = -(-(cap + 2 * held) // 8) * 8
    rows = shards * block
    slots = shards * cap
    size = width // COMPS
    users = shards * held
    params = pltpu.CompilerParams(vmem_limit_bytes=VMEM_LIMIT)

    packed = pl.pallas_call(
        functools.partial(pack_kernel, cap, block),
        out_shape=jax.ShapeDtypeStruct((rows, width), BF16),
        compiler_params=pltpu.CompilerParams(vmem_limit_bytes=PACK_LIMIT),
        name="pack",
    )(item_features, owner.T, table_slot.reshape(1, items), pair_users.T, user_comps, user_gates)
    recv = lax.all_to_all(packed, shard_axes, split_axis=0, concat_axis=0, tiled=True)
    weight_t = tower_weight.T
    table_t = item_table.T

    order = [
        ((z * across + x) * cores, (z * across + x) * cores + 1) for x in range(across) for z in range(deep)
    ]
    half = width // cores
    core = lax.axis_index("core")
    scalar = pl.BlockSpec(memory_space=pltpu.SMEM)
    vmem = pl.BlockSpec(memory_space=pltpu.VMEM)
    own = held * COMPS
    pad = -(-held // 16) * 16
    table_grad, user_part, x_own, x_send, dp_t = pl.pallas_call(
        functools.partial(train_kernel, shards, cap, block, held, order),
        out_shape=(
            jax.ShapeDtypeStruct((item_table.shape[0], width), F32),
            jax.ShapeDtypeStruct((shards, own + pad, size), BF16),
            jax.ShapeDtypeStruct((half, slots), BF16),
            jax.ShapeDtypeStruct((half, slots), BF16),
            jax.ShapeDtypeStruct((width, slots), BF16),
        ),
        in_specs=[scalar, vmem, vmem, vmem],
        scratch_shapes=[
            pltpu.VMEM((users * COMPS, size), F32),
            pltpu.VMEM((COMPS * COMPS, slots), F32),
            pltpu.VMEM((COMPS * COMPS, slots), F32),
            pltpu.VMEM((COMPS * COMPS, slots), F32),
            pltpu.VMEM((COMPS * COMPS, slots), F32),
            pltpu.VMEM((width, slots), F32),
            pltpu.VMEM((width, slots), F32),
            pltpu.VMEM((COMPS, slots), F32),
            pltpu.VMEM((2 * size, COMPS * slots), BF16),
            pltpu.VMEM((users * COMPS, COMPS * slots), BF16),
            pltpu.VMEM((width, slots), BF16),
            pltpu.VMEM((width, slots), BF16),
        ],
        compiler_params=params,
        name="train",
    )(core.reshape(1), recv, weight_t, table_t)

    swap = [(0, 1), (1, 0)]
    x_far = lax.ppermute(x_send, "core", swap)
    dp_far = lax.ppermute(dp_t, "core", swap)
    partners = groups * across
    tall, wide = half // across, width // groups
    parts = pl.pallas_call(
        functools.partial(tower_kernel, groups, across),
        out_shape=blocks(partners, (tall, wide)),
        in_specs=[scalar] + [vmem] * 4,
        compiler_params=params,
        name="tower",
    )(lax.axis_index(("y", "x")).reshape(1), x_own, x_far, dp_t, dp_far)
    got = exchange(parts, ("y", "x"), partners)
    parts = pl.pallas_call(
        functools.partial(sum_kernel, len(got), partners, deep),
        out_shape=blocks(deep, (tall // deep, wide)),
        in_specs=[scalar] + [vmem] * len(got),
        compiler_params=params,
        name="sums",
    )(lax.axis_index("z").reshape(1), *got)
    got = exchange(parts, "z", deep)
    if deep > FEW:
        mine = jnp.sum(got[0].astype(F32), axis=0)
    else:
        mine = sum(part.astype(F32) for part in got)
    if groups == 2:
        other = lax.ppermute(mine, "y", swap)
        first = lax.axis_index("y") == 0
        tower_grad = jnp.concatenate(
            [jnp.where(first, mine, other), jnp.where(first, other, mine)], axis=1
        )
    else:
        tower_grad = lax.all_gather(mine, "y", axis=1, tiled=True)

    got_users = lax.all_to_all(user_part, shard_axes, split_axis=0, concat_axis=0, tiled=True)
    user_sum = jnp.sum(got_users.astype(F32), axis=0)
    user_comp_grad = user_sum[:own].reshape(held, width)
    user_gate_grad = user_sum[own : own + held, : COMPS * COMPS]
    return tower_grad, table_grad, user_comp_grad, user_gate_grad


def solution(mesh):
    groups, shards = mesh.shape["group"], mesh.shape["shard"]
    cores = 2
    chips = shards // cores
    across = 1
    while 8 * across * across <= chips:
        across *= 2
    sizes = (groups, chips // across, across, cores)
    fine = Mesh(np.asarray(mesh.devices).reshape(sizes), ("y", "z", "x", "core"))
    whole = ("y", "z", "x", "core")
    placed = (
        P(whole, None), P(), P(whole, None), P(whole, None),
        P(whole), P(whole, None), P(whole, None), P(whole, None),
    )
    return jax.shard_map(
        functools.partial(local, sizes),
        mesh=fine,
        in_specs=placed,
        out_specs=(
            P(("z", "x", "core"), None), P(whole, None), P(whole, None), P(whole, None),
        ),
        check_vma=False,
    )
```

```python
import functools
import math

import jax
import jax.numpy as jnp
import numpy as np
from jax import lax
from jax.experimental import pallas as pl
from jax.experimental.pallas import tpu as pltpu
from jax.sharding import Mesh, PartitionSpec as P

COMPS = 8
KINDS = 4
LANES = 128
F32 = jnp.float32
BF16 = jnp.bfloat16
VMEM_LIMIT = 24 * 1024 * 1024
PACK_LIMIT = 60 * 1024 * 1024
FEW = 4


def iota(shape, axis):
    return lax.broadcasted_iota(jnp.int32, shape, axis)


def split_by(numbers, size):
    quotient = jnp.floor((numbers.astype(F32) + 0.5) * (1.0 / size)).astype(jnp.int32)
    return quotient, numbers - quotient * size


def nn(a, b):
    return lax.dot_general(a, b, (((1,), (0,)), ((), ())), preferred_element_type=F32)


def nt(a, b):
    return lax.dot_general(a, b, (((1,), (1,)), ((), ())), preferred_element_type=F32)


def halves(values):
    high = values.astype(BF16)
    return high, (values - high.astype(F32)).astype(BF16)


def erf(x):
    x = jnp.clip(x, -3.832506856900711, 3.832506856900711)
    s = x * x
    top = 0.00022905065861350646
    for c in (0.0034082910107109506, 0.050955695062380861, 0.18520832239976145, 1.128379143519084):
        top = top * s + c
    low = -1.1791602954361697e-7
    for c in (
        0.000023547966471313185,
        0.0010179625278914885,
        0.014070470171167667,
        0.11098505178285362,
        0.49746925110067538,
        1.0,
    ):
        low = low * s + c
    return x * top / low


def pack_kernel(cap, block, x_ref, owner_ref, slot_ref, pair_ref, user_ref, gate_ref, out_ref):
    items = x_ref.shape[0]
    rows = out_ref.shape[0]
    held = user_ref.shape[0]
    wide = (items, items)
    own_j = jnp.broadcast_to(owner_ref[...].astype(F32), wide)
    own_i = jnp.transpose(own_j)
    i, j = iota(wide, 0), iota(wide, 1)
    same = own_i == own_j
    rank_row = jnp.sum(jnp.where(same & (i < j), 1.0, 0.0), axis=0, keepdims=True)
    rank_col = jnp.sum(jnp.where(same & (j < i), 1.0, 0.0), axis=1, keepdims=True)

    def column(row):
        return jnp.sum(jnp.where(i == j, row.astype(F32), 0.0), axis=1, keepdims=True)

    slot_col = column(slot_ref[...])
    first_col, second_col = column(pair_ref[0:1, :]), column(pair_ref[1:2, :])
    own_row = own_j[0:1, :]
    row_ids = iota((rows, items), 0)
    place = (own_row * block + rank_row).astype(jnp.int32)
    select = (row_ids == place).astype(F32).astype(BF16)
    _, spot = split_by(iota((rows, held), 0), block)
    lane = iota((rows, held), 1)
    main = nn(select, x_ref[...]) + nn(
        (spot == lane + cap).astype(F32).astype(BF16), user_ref[...]
    )
    width = gate_ref.shape[1]
    padded = nn(
        gate_ref[...], (iota((width, LANES), 0) == iota((width, LANES), 1)).astype(F32).astype(BF16)
    ).astype(BF16)
    gates = nn((spot == lane + cap + held).astype(F32).astype(BF16), padded)
    kind, turn = split_by(iota((items, LANES), 1), cap)
    value = jnp.where(
        kind == 0,
        slot_col,
        jnp.where(kind == 1, first_col, jnp.where(kind == 2, second_col, 1.0)),
    )
    value = jnp.where((kind < KINDS) & (rank_col.astype(jnp.int32) == turn), value, 0.0)
    to_owner = row_ids == (own_row * block + (cap + held)).astype(jnp.int32)
    header = nn(to_owner.astype(F32).astype(BF16), value.astype(BF16))
    out_ref[:, :LANES] = (main[:, :LANES] + gates).astype(BF16)
    out_ref[:, LANES : 2 * LANES] = (main[:, LANES : 2 * LANES] + header).astype(BF16)
    out_ref[:, 2 * LANES :] = main[:, 2 * LANES :].astype(BF16)


def train_kernel(
    shards, cap, block, held, order,
    core_ref, recv_ref, wt_ref, table_t_ref,
    table_grad_ref, user_ref, x_own_ref, x_far_ref, dpt_ref,
    comp_ref, pos_ref, neg_ref, dpos_ref, dneg_ref, norm_ref, slope_ref, scale_ref,
    split_ref, dense_ref, dc_ref, low_ref,
):
    rows, width = recv_ref.shape
    slots = shards * cap
    users = shards * held
    comps = COMPS
    size = width // comps
    tables = table_t_ref.shape[1]
    recv = recv_ref[...]

    def rows_of(count, per, first):
        quotient, rest = split_by(iota((count, rows), 0), per)
        picked = iota((count, rows), 1) == quotient * block + first + rest
        return picked.astype(F32).astype(BF16)

    picked = nn(jnp.concatenate([rows_of(slots, cap, 0), rows_of(users, held, cap)], axis=0), recv)
    x_t = jnp.transpose(picked[:slots].astype(BF16))
    unit = width // shards
    first_core = core_ref[0] == 0
    for place, (here, there) in enumerate(order):
        into = slice(place * unit, (place + 1) * unit)
        one = x_t[here * unit : (here + 1) * unit, :]
        two = x_t[there * unit : (there + 1) * unit, :]
        x_own_ref[into, :] = jnp.where(first_core, one, two)
        x_far_ref[into, :] = jnp.where(first_core, two, one)
    user_rows = picked[slots:]
    for p in range(comps):
        comp_ref[pl.ds(p, users, stride=comps), :] = user_rows[:, p * size : (p + 1) * size]
    comp_rows = comp_ref[...].astype(BF16)
    comp_t = jnp.transpose(comp_ref[...]).astype(BF16)
    gates_t = jnp.transpose(nn(rows_of(users, held, cap + held), recv[:, :LANES]))[: comps * comps]
    pairs = (comps * comps, comps * comps)
    outer, inner = split_by(iota(pairs, 0), comps)
    swap = (iota(pairs, 1) == inner * comps + outer).astype(F32).astype(BF16)
    gates_t = nn(swap, gates_t.astype(BF16)).astype(BF16)

    raw = nn(rows_of(shards, 1, cap + held), recv[:, LANES : 2 * LANES])
    source, turn = split_by(iota((shards, slots), 1), cap)
    spread = (source == iota((shards, slots), 0)).astype(F32).astype(BF16)
    fields = nn(jnp.transpose(raw).astype(BF16), spread)
    kind, field_turn = split_by(iota((LANES, slots), 0), cap)
    _, slot_turn = split_by(iota((LANES, slots), 1), cap)
    fields = jnp.where(field_turn == slot_turn, fields, 0.0)

    def field(number):
        return jnp.sum(jnp.where(kind == number, fields, 0.0), axis=0, keepdims=True)

    table_row = field(0).astype(jnp.int32)
    pos_row = field(1).astype(jnp.int32)
    neg_row = field(2).astype(jnp.int32)
    present = field(3)
    pick_table = (iota((tables, slots), 0) == table_row).astype(F32).astype(BF16)
    user_ids = iota((users, slots), 0)
    gate_pos = nn(gates_t, (user_ids == pos_row).astype(F32).astype(BF16))
    gate_neg = nn(gates_t, (user_ids == neg_row).astype(F32).astype(BF16))
    comp_twice = jnp.concatenate([comp_rows, comp_rows], axis=1)
    ids3 = iota((users, comps, slots), 0)
    is_pos = ids3 == pos_row[None]
    is_neg = ids3 == neg_row[None]

    slope_ref[...] = nn(wt_ref[...], x_t)
    norm_ref[...] = nn(table_t_ref[...], pick_table)
    for q in range(comps):
        part, wide = slice(q * size, (q + 1) * size), slice(q * slots, (q + 1) * slots)
        pre = slope_ref[part, :]
        share = 0.5 + 0.5 * erf(pre * math.sqrt(0.5))
        slope_ref[part, :] = share + pre * (jnp.exp(-0.5 * pre * pre) * (1.0 / math.sqrt(2.0 * math.pi)))
        combined = (pre * share).astype(BF16).astype(F32) + norm_ref[part, :]
        scale = lax.rsqrt(jnp.mean(combined * combined, axis=0, keepdims=True) + 1e-06)
        scale_ref[q : q + 1, :] = scale
        normed = combined * scale
        norm_ref[part, :] = normed
        high, low = halves(normed)
        split_ref[:size, wide] = high
        split_ref[size:, wide] = low
        logits = nn(comp_twice, split_ref[:, wide]).reshape(users, comps, slots)
        pos_ref[q * comps : (q + 1) * comps, :] = jnp.sum(jnp.where(is_pos, logits, 0.0), axis=0)
        neg_ref[q * comps : (q + 1) * comps, :] = jnp.sum(jnp.where(is_neg, logits, 0.0), axis=0)

    def side(logits, gates, sign):
        weights = jax.nn.sigmoid(gates + logits)
        score = 0.125 * jnp.sum(weights * logits, axis=0, keepdims=True)
        d_score = 0.125 * sign * jax.nn.sigmoid(sign * score) * present
        d_gates = d_score * (logits * weights * (1.0 - weights))
        return d_gates + d_score * weights, d_gates

    d_pos, dg_pos = side(pos_ref[...], gate_pos, -1.0)
    d_neg, dg_neg = side(neg_ref[...], gate_neg, 1.0)
    dpos_ref[...] = d_pos
    dneg_ref[...] = d_neg

    pad = user_ref.shape[1] - held * comps
    mate, rest = split_by(iota((shards * pad, slots), 0), pad)
    person = jnp.where(rest < held, mate * held + rest, -1)
    mask_pos = (person == pos_row).astype(F32).astype(BF16)
    mask_neg = (person == neg_row).astype(F32).astype(BF16)
    d_gate = jnp.zeros((shards * pad, comps * comps), F32)
    for mask, values in ((mask_pos, dg_pos), (mask_neg, dg_neg)):
        for piece in halves(values):
            d_gate = d_gate + nt(mask, nn(swap, piece).astype(BF16))
    own = held * comps
    user_ref[:, own:, : comps * comps] = d_gate.reshape(shards, pad, comps * comps).astype(BF16)
    user_ref[:, own:, comps * comps :] = jnp.zeros(
        (shards, pad, size - comps * comps), BF16
    )

    for q in range(comps):
        wide = slice(q * slots, (q + 1) * slots)
        d_logit_pos = dpos_ref[q * comps : (q + 1) * comps, :][None]
        d_logit_neg = dneg_ref[q * comps : (q + 1) * comps, :][None]
        dense = jnp.where(is_pos, d_logit_pos, 0.0) + jnp.where(is_neg, d_logit_neg, 0.0)
        dense_high, dense_low = halves(dense.reshape(users * comps, slots))
        dense_ref[:, wide] = dense_high
        part = slice(q * size, (q + 1) * size)
        normed = norm_ref[part, :]
        d_normed = nn(comp_t, dense_high) + nn(comp_t, dense_low)
        inner = jnp.mean(d_normed * normed, axis=0, keepdims=True)
        d_combined = scale_ref[q : q + 1, :] * (d_normed - normed * inner)
        d_embedded = d_combined.astype(BF16)
        dpt_ref[part, :] = (d_embedded.astype(F32) * slope_ref[part, :]).astype(BF16)
        dc_ref[part, :] = d_embedded
        low_ref[part, :] = (d_combined - d_embedded.astype(F32)).astype(BF16)
    d_users = nt(dense_ref[...], split_ref[...])
    d_users = d_users[:, :size] + d_users[:, size:]
    user_ref[:, :own, :] = d_users.reshape(shards, own, size).astype(BF16)
    table_grad_ref[...] = nt(pick_table, dc_ref[...]) + nt(pick_table, low_ref[...])


def views(refs, count):
    return list(refs) if len(refs) == count else [refs[0].at[k] for k in range(count)]


def blocks(count, shape):
    if count <= FEW:
        return [jax.ShapeDtypeStruct(shape, BF16)] * count
    return [jax.ShapeDtypeStruct((count,) + shape, BF16)]


def partner_of(me_ref, k, count):
    return me_ref[0] ^ k if count <= FEW else k


def exchange(parts, axis, count):
    if count > FEW:
        return [lax.all_to_all(parts[0], axis, split_axis=0, concat_axis=0, tiled=True)]
    return [parts[0]] + [
        lax.ppermute(parts[k], axis, [(i, i ^ k) for i in range(count)]) for k in range(1, count)
    ]


def tower_kernel(groups, across, me_ref, x_ref, x_far_ref, d_ref, d_far_ref, *outs):
    wide = d_ref.shape[0] // groups
    tall = x_ref.shape[0] // across
    count = groups * across
    for k, out_ref in enumerate(views(outs, count)):
        partner = partner_of(me_ref, k, count)
        tower_rows = pl.ds(pl.multiple_of(lax.rem(partner, across) * tall, tall), tall)
        columns = pl.ds(pl.multiple_of(lax.div(partner, across) * wide, wide), wide)
        out_ref[...] = (
            nt(x_ref[tower_rows, :], d_ref[columns, :]) + nt(x_far_ref[tower_rows, :], d_far_ref[columns, :])
        ).astype(BF16)


def sum_kernel(given, count, deep, me_ref, *refs):
    ins, outs = views(refs[:given], count), views(refs[given:], deep)
    tall = outs[0].shape[0]
    for k, out_ref in enumerate(outs):
        part = pl.ds(pl.multiple_of(partner_of(me_ref, k, deep) * tall, tall), tall)
        total = ins[0][part, :].astype(F32)
        for in_ref in ins[1:]:
            total = total + in_ref[part, :].astype(F32)
        out_ref[...] = total.astype(BF16)


def local(
    sizes, item_features, tower_weight, item_table, owner, table_slot, pair_users, user_comps, user_gates
):
    groups, deep, across, cores = sizes
    shards = deep * across * cores
    shard_axes = ("z", "x", "core")
    items, width = item_features.shape
    cap = max(1, 2 * items // shards)
    held = user_comps.shape[0]
    block = -(-(cap + 2 * held) // 8) * 8
    rows = shards * block
    slots = shards * cap
    size = width // COMPS
    users = shards * held
    params = pltpu.CompilerParams(vmem_limit_bytes=VMEM_LIMIT)

    packed = pl.pallas_call(
        functools.partial(pack_kernel, cap, block),
        out_shape=jax.ShapeDtypeStruct((rows, width), BF16),
        compiler_params=pltpu.CompilerParams(vmem_limit_bytes=PACK_LIMIT),
        name="pack",
    )(item_features, owner.T, table_slot.reshape(1, items), pair_users.T, user_comps, user_gates)
    recv = lax.all_to_all(packed, shard_axes, split_axis=0, concat_axis=0, tiled=True)
    weight_t = tower_weight.T
    table_t = item_table.T

    order = [
        ((z * across + x) * cores, (z * across + x) * cores + 1) for x in range(across) for z in range(deep)
    ]
    half = width // cores
    core = lax.axis_index("core")
    scalar = pl.BlockSpec(memory_space=pltpu.SMEM)
    vmem = pl.BlockSpec(memory_space=pltpu.VMEM)
    own = held * COMPS
    pad = -(-held // 16) * 16
    table_grad, user_part, x_own, x_send, dp_t = pl.pallas_call(
        functools.partial(train_kernel, shards, cap, block, held, order),
        out_shape=(
            jax.ShapeDtypeStruct((item_table.shape[0], width), F32),
            jax.ShapeDtypeStruct((shards, own + pad, size), BF16),
            jax.ShapeDtypeStruct((half, slots), BF16),
            jax.ShapeDtypeStruct((half, slots), BF16),
            jax.ShapeDtypeStruct((width, slots), BF16),
        ),
        in_specs=[scalar, vmem, vmem, vmem],
        scratch_shapes=[
            pltpu.VMEM((users * COMPS, size), F32),
            pltpu.VMEM((COMPS * COMPS, slots), F32),
            pltpu.VMEM((COMPS * COMPS, slots), F32),
            pltpu.VMEM((COMPS * COMPS, slots), F32),
            pltpu.VMEM((COMPS * COMPS, slots), F32),
            pltpu.VMEM((width, slots), F32),
            pltpu.VMEM((width, slots), F32),
            pltpu.VMEM((COMPS, slots), F32),
            pltpu.VMEM((2 * size, COMPS * slots), BF16),
            pltpu.VMEM((users * COMPS, COMPS * slots), BF16),
            pltpu.VMEM((width, slots), BF16),
            pltpu.VMEM((width, slots), BF16),
        ],
        compiler_params=params,
        name="train",
    )(core.reshape(1), recv, weight_t, table_t)

    swap = [(0, 1), (1, 0)]
    x_far = lax.ppermute(x_send, "core", swap)
    dp_far = lax.ppermute(dp_t, "core", swap)
    partners = groups * across
    tall, wide = half // across, width // groups
    parts = pl.pallas_call(
        functools.partial(tower_kernel, groups, across),
        out_shape=blocks(partners, (tall, wide)),
        in_specs=[scalar] + [vmem] * 4,
        compiler_params=params,
        name="tower",
    )(lax.axis_index(("y", "x")).reshape(1), x_own, x_far, dp_t, dp_far)
    got = exchange(parts, ("y", "x"), partners)
    parts = pl.pallas_call(
        functools.partial(sum_kernel, len(got), partners, deep),
        out_shape=blocks(deep, (tall // deep, wide)),
        in_specs=[scalar] + [vmem] * len(got),
        compiler_params=params,
        name="sums",
    )(lax.axis_index("z").reshape(1), *got)
    got = exchange(parts, "z", deep)
    if deep > FEW:
        mine = jnp.sum(got[0].astype(F32), axis=0)
    else:
        mine = sum(part.astype(F32) for part in got)
    if groups == 2:
        other = lax.ppermute(mine, "y", swap)
        first = lax.axis_index("y") == 0
        tower_grad = jnp.concatenate(
            [jnp.where(first, mine, other), jnp.where(first, other, mine)], axis=1
        )
    else:
        tower_grad = lax.all_gather(mine, "y", axis=1, tiled=True)

    got_users = lax.all_to_all(user_part, shard_axes, split_axis=0, concat_axis=0, tiled=True)
    user_sum = jnp.sum(got_users.astype(F32), axis=0)
    user_comp_grad = user_sum[:own].reshape(held, width)
    user_gate_grad = user_sum[own : own + held, : COMPS * COMPS]
    return tower_grad, table_grad, user_comp_grad, user_gate_grad


def solution(mesh):
    groups, shards = mesh.shape["group"], mesh.shape["shard"]
    cores = 2
    chips = shards // cores
    across = 1
    while 8 * across * across <= chips:
        across *= 2
    sizes = (groups, chips // across, across, cores)
    fine = Mesh(np.asarray(mesh.devices).reshape(sizes), ("y", "z", "x", "core"))
    whole = ("y", "z", "x", "core")
    placed = (
        P(whole, None), P(), P(whole, None), P(whole, None),
        P(whole), P(whole, None), P(whole, None), P(whole, None),
    )
    return jax.shard_map(
        functools.partial(local, sizes),
        mesh=fine,
        in_specs=placed,
        out_specs=(
            P(("z", "x", "core"), None), P(whole, None), P(whole, None), P(whole, None),
        ),
        check_vma=False,
    )
```
